256 devices in a mesh: group: 32 (over y, z), local: 8 (over x, core).
Axes of the slice: x: 4, y: 4, z: 8, core: 2. Of those that a mesh axis runs over, the one named last changes fastest.
Arguments:
- tokens: bfloat16 [2048, 7168], P('group', 'local'), may hold values from -6 to 6
- routes: int32 [2048, 8], P('group'), may hold values from 0 to 31, as said below
- affinity: float32 [2048, 8], P('group'), may hold values from 0.05 to 0.6
- gate_proj: bfloat16 [32, 7168, 2048], P('group', None, 'local'), may hold values from -0.0625 to 0.0625
- up_proj: bfloat16 [32, 7168, 2048], P('group', None, 'local'), may hold values from -0.0625 to 0.0625
- down_proj: bfloat16 [32, 2048, 7168], P('group', None, 'local'), may hold values from -0.125 to 0.125
Outputs:
- combined: bfloat16 [2048, 7168], P('group', 'local')
The draws below stay inside these ranges and needn't reach their ends.
Inputs may be any that keep to these rules, and one draw needn't show every extreme that they name: `routes`: each token names 8 distinct experts, two in each of 4 node groups (node group n holds experts n * 4 to (n + 1) * 4 - 1); in each block of 64 tokens every node group is named by exactly half of the tokens, no expert is named by more than 24 tokens, and one expert of every node group, the same in all blocks, is named by exactly 24 tokens of every block.
All inputs are finite; a program needn't handle non-finite values.
Results may differ from the reference program's by a relative error of at most 0.0058.
Values may be sent and summed in bfloat16 or wider, within the bound.
A program may use at most 64 MiB of HBM per device.

```python
import math
import jax
import jax.numpy as jnp
from jax import lax

D = 7168
HID = 2048
TOP = 8
NODE_GROUPS = 8
NODE_LIMIT = 4
TOK_G = 64
TOKENS = 2048
EXPERTS = 32
EPN = 4
CAP = 24
N_GROUP = 32


def quota_table():
    remaining = TOK_G - CAP
    others = EPN - 1
    even_share = remaining // others
    leftover = remaining % others
    swing = TOK_G * TOP // (4 * EXPERTS)
    quotas = []
    for position in range(1, EPN):
        amount = even_share + (1 if position - 1 < leftover else 0)
        if position % 2 == 1 and position + 1 <= others:
            amount = amount + swing
        elif position % 2 == 0:
            amount = amount - swing
        quotas.append(amount)
    return quotas


def draw_routes(key, part):
    key = jax.random.fold_in(key, 17)
    blocks = TOKENS // TOK_G
    half_block = TOK_G // 2
    key_rank, key_shift, key_subset, key_full, key_order = jax.random.split(key, 5)
    token_axis = jnp.arange(TOK_G, dtype=jnp.int32)
    group_axis = jnp.arange(NODE_GROUPS, dtype=jnp.int32)
    rank_scores = jax.random.randint(key_rank, (blocks, TOK_G), 0, 4096, dtype=jnp.int32) * TOK_G + token_axis[None, :]
    ranking = jnp.argsort(jnp.argsort(rank_scores, axis=1), axis=1).astype(jnp.int32)
    shifts = jax.random.randint(key_shift, (blocks, 1, 1), 0, NODE_GROUPS, dtype=jnp.int32)
    subset_scores = jax.random.randint(key_subset, (blocks, NODE_GROUPS), 0, 1024, dtype=jnp.int32) * NODE_GROUPS + group_axis[None, :]
    picked_offsets = jnp.argsort(subset_scores, axis=1)[:, :NODE_LIMIT].astype(jnp.int32)
    member = jnp.sum((picked_offsets[:, :, None] == group_axis[None, None, :]).astype(jnp.int32), axis=1)
    offsets = (group_axis[None, None, :] - shifts - token_axis[None, :, None]) % NODE_GROUPS
    picks = jnp.sum((offsets[:, :, :, None] == group_axis[None, None, None, :]).astype(jnp.int32) * member[:, None, None, :], axis=3)
    within = jnp.cumsum(picks, axis=1) - picks
    full_local = jax.random.randint(key_full, (1, NODE_GROUPS, 1), 0, EPN, dtype=jnp.int32)
    shuffle_scores = jax.random.randint(key_order, (blocks, NODE_GROUPS, EPN - 1), 0, 1024, dtype=jnp.int32) * (EPN - 1) + jnp.arange(EPN - 1, dtype=jnp.int32)[None, None, :]
    shuffled = jnp.argsort(shuffle_scores, axis=2).astype(jnp.int32)
    rest_quotas = jnp.array(quota_table(), dtype=jnp.int32)
    shuffled_quotas = rest_quotas[shuffled]
    expert_axis = jnp.arange(EPN, dtype=jnp.int32)[None, None, :]
    other_index = jnp.clip(expert_axis - (expert_axis > full_local).astype(jnp.int32), 0, EPN - 2)
    other_index = jnp.broadcast_to(other_index, (blocks, NODE_GROUPS, EPN))
    quota = jnp.where(expert_axis == full_local, CAP, jnp.take_along_axis(shuffled_quotas, other_index, axis=2))
    bounds = jnp.cumsum(quota, axis=2)
    first_local = jnp.sum((bounds[:, None, :, :] <= within[:, :, :, None]).astype(jnp.int32), axis=3)
    second_local = jnp.sum((bounds[:, None, :, :] <= within[:, :, :, None] + half_block).astype(jnp.int32), axis=3)
    chosen_groups = (shifts + token_axis[None, :, None] + picked_offsets[:, None, :]) % NODE_GROUPS
    firsts = jnp.take_along_axis(first_local, chosen_groups, axis=2)
    seconds = jnp.take_along_axis(second_local, chosen_groups, axis=2)
    identities = jnp.concatenate([chosen_groups * EPN + firsts, chosen_groups * EPN + seconds], axis=2)
    rank_index = jnp.broadcast_to(ranking[:, :, None], (blocks, TOK_G, TOP))
    by_token = jnp.take_along_axis(identities, rank_index, axis=1)
    return by_token.reshape(TOKENS, TOP).astype(jnp.int32)


def level_of(key, dims, cuts, least, largest):
    factor_of, own = 1.0, jax.random.fold_in(key, 6)
    for axis_at, parts in cuts:
        steps = jnp.exp(jax.random.uniform(jax.random.fold_in(own, axis_at), (parts,), jnp.float32, least / len(cuts), largest / len(cuts)))
        factor_of = factor_of * jnp.repeat(steps, dims[axis_at] // parts).reshape([-1 if axis == axis_at else 1 for axis in range(len(dims))])
    return factor_of


def noise(rng, dims, deviation, bound, pieces=(), kind=jnp.bfloat16):
    drawn = jax.random.normal(rng, dims, jnp.float32) * deviation
    if len(pieces) > 0:
        drawn = level_of(rng, dims, pieces, -0.22, 0.18) * drawn
    return jnp.clip(drawn, min=-bound, max=bound).astype(kind)


def setup_inputs(seed: int = 0) -> dict:
    splits = jax.random.split(jax.random.key(seed), 7)
    return {
        "tokens": noise(splits[0], (TOKENS, D), 1.0, 6.0, ((0, 32), (1, 8))),
        "routes": draw_routes(jax.random.fold_in(splits[6], 71), 0),
        "affinity": jnp.clip(jnp.exp(math.log(0.6) - 2.4849067 * jax.random.uniform(splits[2], (TOKENS, TOP), jnp.float32) ** level_of(splits[2], (TOKENS, TOP), ((0, 32),), -0.2, 0.2)), 0.05, 0.6),
        "gate_proj": noise(splits[3], (EXPERTS, D, HID), D ** -0.5, 0.0625, ((0, 32), (2, 8))),
        "up_proj": noise(splits[4], (EXPERTS, D, HID), D ** -0.5, 0.0625, ((0, 32), (2, 8))),
        "down_proj": noise(splits[5], (EXPERTS, HID, D), HID ** -0.5, 0.125, ((0, 32), (2, 8))),
    }


def block_slots(routes_block, experts):
    chosen = (routes_block[:, :, None] == jnp.arange(experts, dtype=jnp.int32)[None, None, :]).astype(jnp.int32)
    per_token = jnp.sum(chosen, axis=1)
    earlier = jnp.cumsum(per_token, axis=0) - per_token
    return jnp.sum(chosen * earlier[:, None, :], axis=2).astype(jnp.int32)


def slot_owner(routes_block, slot_index, capacity, experts):
    flat_slot = (routes_block * capacity + slot_index).reshape(-1).astype(jnp.int32)
    token_ids = jnp.broadcast_to(jnp.arange(routes_block.shape[0], dtype=jnp.int32)[:, None], routes_block.shape).reshape(-1)
    owner_table = jnp.full((experts * capacity,), -1, dtype=jnp.int32)
    return owner_table.at[flat_slot].set(token_ids)


def take_rows(block_tokens, index_rows):
    return block_tokens[index_rows]


def reference(tokens, routes, affinity, gate_proj, up_proj, down_proj):
    experts = EXPERTS
    route_blocks = routes.reshape(N_GROUP, TOK_G, TOP)
    token_blocks = tokens.reshape(N_GROUP, TOK_G, D)

    def slots_of(routes_block):
        return block_slots(routes_block, experts)

    slot_blocks = jax.vmap(slots_of)(route_blocks)

    def owners_of(routes_block, slot_block):
        return slot_owner(routes_block, slot_block, CAP, experts)

    owners = jax.vmap(owners_of)(route_blocks, slot_blocks)

    def run_expert(inputs):
        expert_id, gate_matrix, up_matrix, down_matrix = inputs
        owner_cols = lax.dynamic_slice_in_dim(owners, (expert_id * CAP).astype(jnp.int32), CAP, 1)
        rows = jax.vmap(take_rows)(token_blocks, jnp.maximum(owner_cols, 0))
        rows = jnp.where((owner_cols >= 0)[:, :, None], rows, jnp.zeros((), rows.dtype))
        rows = rows.reshape(N_GROUP * CAP, D)
        gate_pre = jnp.dot(rows, gate_matrix, preferred_element_type=jnp.float32)
        up_pre = jnp.dot(rows, up_matrix, preferred_element_type=jnp.float32)
        hidden = (jax.nn.silu(gate_pre) * up_pre).astype(jnp.bfloat16)
        result = jnp.dot(hidden, down_matrix, preferred_element_type=jnp.float32).astype(jnp.bfloat16)
        return result.reshape(N_GROUP, CAP, D)

    expert_out = lax.map(run_expert, (jnp.arange(experts, dtype=jnp.int32), gate_proj, up_proj, down_proj))
    slot_flat = slot_blocks.reshape(TOKENS, TOP)
    block_of = jnp.arange(TOKENS, dtype=jnp.int32) // TOK_G
    accumulated = jnp.zeros((TOKENS, D), jnp.float32)
    for column in range(TOP):
        picked = expert_out[routes[:, column], block_of, slot_flat[:, column]]
        accumulated = accumulated + affinity[:, column:column + 1] * picked.astype(jnp.float32)
    return accumulated.astype(jnp.bfloat16)
```

```python
import jax
import jax.numpy as jnp
from jax import lax
from jax.experimental import pallas as pl
from jax.experimental.pallas import tpu as pltpu
from jax.sharding import PartitionSpec as P

MESH = pl.DeviceIdType.MESH
F32, BF16 = jnp.float32, jnp.bfloat16

NY, NZ, NX = 4, 8, 4
GROUPS = NY * NZ
TOK, TOP, CAP = 64, 8, 24
FEAT, HPART = 896, 256
DEV = 2 * NX
ROWS = GROUPS * CAP
CHUNKS = NZ
CROWS = NY * CAP
HALF = CROWS // 2
DISTANCE = (1, 7, 4, 3, 5, 2, 6, 0)
AHEAD = 2

RIGHT, LEFT, RIGHT2, LEFT2, SIB_OWN, SIB_LEFT, SIB_RIGHT, SIB_FAR = range(8)


def distance_of(chunk):
    found = 0
    for index, value in enumerate(DISTANCE):
        if value:
            found = found + jnp.where(chunk == index, value, 0)
    return found


def kernel(
    tokens_ref, routes_ref, affinity_ref, gate_hbm, up_hbm, down_hbm, out_ref,
    gate_ref, up_ref, down_ref, outgoing, landed, rows, hidden, results, returned, weight_of, total,
    weight_sem, self_sem, sent_sem, landed_sem, back_sem, returned_sem, x_send, x_recv, h_send, h_recv,
):
    me_g, me_l = lax.axis_index("group"), lax.axis_index("local")
    y, z = me_g // NZ, lax.rem(me_g, NZ)
    x, core = me_l // 2, lax.rem(me_l, 2)
    right = lax.rem(x + 1, NX) * 2 + core
    left = lax.rem(x + NX - 1, NX) * 2 + core
    far = lax.rem(x + 2, NX) * 2 + core
    sibling = x * 2 + 1 - core

    def group_at(dy, dz):
        return lax.rem(y + dy, NY) * NZ + lax.rem(z + dz, NZ)

    barrier = pltpu.get_barrier_semaphore()

    def greet(offset, carry):
        pl.semaphore_signal(
            barrier, inc=1, device_id=(lax.rem(me_g + offset, GROUPS), me_l), device_id_type=MESH
        )
        return carry

    lax.fori_loop(1, GROUPS, greet, 0)
    for peer in (right, left, sibling):
        pl.semaphore_signal(barrier, inc=1, device_id=(me_g, peer), device_id_type=MESH)

    weights = [
        pltpu.make_async_copy(source.at[0], target, weight_sem.at[index])
        for index, (source, target) in enumerate(
            ((gate_hbm, gate_ref), (up_hbm, up_ref), (down_hbm, down_ref))
        )
    ]
    for copy in weights:
        copy.start()

    block = lax.broadcasted_iota(jnp.int32, (GROUPS, TOK), 0)
    dz_of = distance_of(block // NY)
    dy_of = block - (block // NY) * NY
    yy, zz = y + NY - dy_of, z + NZ - dz_of
    yy = jnp.where(yy >= NY, yy - NY, yy)
    zz = jnp.where(zz >= NZ, zz - NZ, zz)
    expert = yy * NZ + zz
    named = jnp.zeros((GROUPS, TOK), F32)
    gates = jnp.zeros((GROUPS, TOK), F32)
    for k in range(TOP):
        same = routes_ref[k : k + 1, :] == expert
        named = named + jnp.where(same, 1.0, 0.0)
        gates = gates + jnp.where(same, affinity_ref[k : k + 1, :], 0.0)
    before = lax.broadcasted_iota(jnp.int32, (TOK, TOK), 0) < lax.broadcasted_iota(jnp.int32, (TOK, TOK), 1)
    earlier = jnp.dot(named.astype(BF16), jnp.where(before, 1.0, 0.0).astype(BF16), preferred_element_type=F32)
    slot = jnp.where(named > 0.5, earlier, -1.0).astype(jnp.int32)
    place = lax.broadcasted_iota(jnp.int32, (GROUPS, CAP, TOK), 1)
    holds = slot[:, None, :] == place
    pick = jnp.where(holds, 1.0, 0.0).reshape(ROWS, TOK).astype(BF16)
    for at in range(0, GROUPS, 8):
        part = jnp.dot(pick[at * CAP : (at + 8) * CAP], tokens_ref[...], preferred_element_type=F32)
        outgoing[at : at + 8] = part.reshape(8, CAP, FEAT).astype(BF16)

    pl.semaphore_wait(barrier, GROUPS - 1 + 3)

    own = DISTANCE.index(0) * NY
    own_chunk = own // NY
    self_copy = pltpu.make_async_copy(outgoing.at[own], landed.at[own], self_sem.at[0])
    self_copy.start()

    def dispatch(s, carry):
        dz, dy = distance_of(s // NY), lax.rem(s, NY)

        @pl.when(s != own)
        def _():
            pltpu.make_async_remote_copy(
                src_ref=outgoing.at[s],
                dst_ref=landed.at[s],
                send_sem=sent_sem.at[0],
                recv_sem=landed_sem.at[s],
                device_id=(group_at(NY - dy, NZ - dz), me_l),
                device_id_type=MESH,
            ).start()

        return carry

    lax.fori_loop(0, GROUPS, dispatch, 0)

    spread = jnp.where(holds, gates[:, None, :], 0.0).reshape(ROWS, TOK)
    high = spread.astype(BF16)
    low = (spread - high.astype(F32)).astype(BF16)
    weight_of[...] = jnp.concatenate([high.astype(F32), low.astype(F32)], axis=1).reshape(
        CHUNKS, CROWS, 2 * TOK
    )
    total[...] = jnp.zeros_like(total)

    def ring(buffer, send, recv, kind, chunk):
        start = pl.multiple_of(chunk * CROWS, CROWS)
        slot_of, begin, count, target = {
            RIGHT: (me_l, 0, CROWS, right),
            LEFT: (me_l, 0, CROWS, left),
            RIGHT2: (left, 0, HALF, right),
            LEFT2: (right, HALF, HALF, left),
            SIB_OWN: (me_l, 0, CROWS, sibling),
            SIB_LEFT: (left, 0, CROWS, sibling),
            SIB_RIGHT: (right, 0, CROWS, sibling),
            SIB_FAR: (far, 0, CROWS, sibling),
        }[kind]
        piece = buffer.at[slot_of, pl.ds(start + begin, count)]
        return pltpu.make_async_remote_copy(
            src_ref=piece,
            dst_ref=piece,
            send_sem=send.at[kind, chunk],
            recv_sem=recv.at[kind, chunk],
            device_id=(me_g, target),
            device_id_type=MESH,
        )

    def x_ring(kind, chunk):
        return ring(rows, x_send, x_recv, kind, chunk)

    def h_ring(kind, chunk):
        return ring(hidden, h_send, h_recv, kind, chunk)

    def begin_rows(chunk):
        for dy in range(NY):
            s = chunk * NY + dy

            @pl.when(s != own)
            def _():
                pltpu.make_async_copy(landed.at[s], landed.at[s], landed_sem.at[s]).wait()

            if dy == 0:

                @pl.when(s == own)
                def _():
                    self_copy.wait()

        blocks = landed[pl.ds(chunk * NY, NY)].astype(F32).reshape(CROWS, FEAT).astype(BF16)
        rows[me_l, pl.ds(pl.multiple_of(chunk * CROWS, CROWS), CROWS)] = blocks
        for kind in (RIGHT, LEFT, SIB_OWN):
            x_ring(kind, chunk).start()

    def second(make, chunk):
        make(RIGHT, chunk).wait_recv()
        make(RIGHT2, chunk).start()
        make(SIB_LEFT, chunk).start()
        make(LEFT, chunk).wait_recv()
        make(LEFT2, chunk).start()
        make(SIB_RIGHT, chunk).start()

    def third(make, chunk):
        make(RIGHT2, chunk).wait_recv()
        make(LEFT2, chunk).wait_recv()
        make(SIB_FAR, chunk).start()

    def gathered(make, chunk):
        for kind in (SIB_OWN, SIB_LEFT, SIB_RIGHT, SIB_FAR):
            make(kind, chunk).wait_recv()

    def hidden_rows(chunk):
        here = pl.ds(pl.multiple_of(chunk * CROWS, CROWS), CROWS)
        gate = jnp.zeros((CROWS, HPART), F32)
        up = jnp.zeros((CROWS, HPART), F32)
        for pair in range(NX):
            lhs = jnp.concatenate([rows[2 * pair, here], rows[2 * pair + 1, here]], axis=1)
            depth = slice(pair * 2 * FEAT, (pair + 1) * 2 * FEAT)
            gate = gate + jnp.dot(lhs, gate_ref[depth, :], preferred_element_type=F32)
            up = up + jnp.dot(lhs, up_ref[depth, :], preferred_element_type=F32)
        value = gate / (1.0 + jnp.exp(-gate)) * up
        hidden[me_l, here] = value.astype(BF16)

    def output_rows(chunk):
        here = pl.ds(pl.multiple_of(chunk * CROWS, CROWS), CROWS)
        lhs = jnp.concatenate([hidden[part, here] for part in range(DEV)], axis=1)
        value = jnp.dot(lhs, down_ref[...], preferred_element_type=F32)
        results[pl.ds(chunk * NY, NY)] = value.reshape(NY, CAP, FEAT).astype(BF16)

    def send_back(chunk):
        dz = distance_of(chunk)
        for dy in range(NY):
            s = chunk * NY + dy

            @pl.when(s != own)
            def _():
                pltpu.make_async_remote_copy(
                    src_ref=results.at[s],
                    dst_ref=returned.at[s],
                    send_sem=back_sem.at[0],
                    recv_sem=returned_sem.at[s],
                    device_id=(group_at(dy, dz), me_l),
                    device_id_type=MESH,
                ).start()

            if dy == 0:

                @pl.when(s == own)
                def _():
                    pltpu.make_async_copy(results.at[s], returned.at[s], self_sem.at[1]).start()

    def combine(chunk):
        for dy in range(NY):
            s = chunk * NY + dy

            @pl.when(s != own)
            def _():
                pltpu.make_async_copy(returned.at[s], returned.at[s], returned_sem.at[s]).wait()

            if dy == 0:

                @pl.when(s == own)
                def _():
                    pltpu.make_async_copy(results.at[s], returned.at[s], self_sem.at[1]).wait()

        values = returned[pl.ds(chunk * NY, NY)].astype(F32).reshape(CROWS, FEAT).astype(BF16)
        both = lax.dot_general(
            weight_of[chunk].astype(BF16), values, (((0,), (0,)), ((), ())), preferred_element_type=F32
        )
        total[...] += both[:TOK] + both[TOK:]

    def early(chunk, carry):
        begin_rows(chunk)
        return carry

    lax.fori_loop(0, AHEAD, early, 0)

    def turn(i, carry):
        @pl.when(i < CHUNKS)
        def _():
            second(x_ring, i)

        @pl.when(i + AHEAD < CHUNKS)
        def _():
            begin_rows(i + AHEAD)

        @pl.when(i >= 1)
        def _():
            second(h_ring, i - 1)

        @pl.when(i < CHUNKS)
        def _():
            third(x_ring, i)

        @pl.when(i >= 1)
        def _():
            third(h_ring, i - 1)

        @pl.when(i == 0)
        def _():
            weights[0].wait()
            weights[1].wait()

        @pl.when(i < CHUNKS)
        def _():
            gathered(x_ring, i)
            hidden_rows(i)
            for kind in (RIGHT, LEFT, SIB_OWN):
                h_ring(kind, i).start()

        @pl.when(i == 1)
        def _():
            weights[2].wait()

        @pl.when(i >= 1)
        def _():
            gathered(h_ring, i - 1)
            output_rows(i - 1)
            send_back(i - 1)

        return carry

    lax.fori_loop(0, CHUNKS + 1, turn, 0)

    def collect(chunk, carry):
        combine(chunk)
        return carry

    lax.fori_loop(0, CHUNKS, collect, 0)
    out_ref[...] = total[...].astype(BF16)

    def settle(chunk, carry):
        for kind in range(8):
            x_ring(kind, chunk).wait_send()
            h_ring(kind, chunk).wait_send()
        return carry

    lax.fori_loop(0, CHUNKS, settle, 0)
    others = pl.ds(0, GROUPS - 1)
    pltpu.make_async_copy(outgoing.at[others], outgoing.at[others], sent_sem.at[0]).wait()
    pltpu.make_async_copy(results.at[others], results.at[others], back_sem.at[0]).wait()


def on_device(tokens, routes, affinity, gate_proj, up_proj, down_proj):
    vmem, anywhere = pl.BlockSpec(memory_space=pltpu.VMEM), pl.BlockSpec(memory_space=pl.ANY)
    dma = pltpu.SemaphoreType.DMA
    return pl.pallas_call(
        kernel,
        out_shape=jax.ShapeDtypeStruct((TOK, FEAT), BF16),
        in_specs=[vmem, vmem, vmem, anywhere, anywhere, anywhere],
        out_specs=vmem,
        scratch_shapes=[
            pltpu.VMEM((DEV * FEAT, HPART), BF16),
            pltpu.VMEM((DEV * FEAT, HPART), BF16),
            pltpu.VMEM((DEV * HPART, FEAT), BF16),
            pltpu.VMEM((GROUPS, CAP, FEAT), BF16),
            pltpu.VMEM((GROUPS, CAP, FEAT), BF16),
            pltpu.VMEM((DEV, ROWS, FEAT), BF16),
            pltpu.VMEM((DEV, ROWS, HPART), BF16),
            pltpu.VMEM((GROUPS, CAP, FEAT), BF16),
            pltpu.VMEM((GROUPS, CAP, FEAT), BF16),
            pltpu.VMEM((CHUNKS, CROWS, 2 * TOK), F32),
            pltpu.VMEM((TOK, FEAT), F32),
            dma((3,)),
            dma((2,)),
            dma((1,)),
            dma((GROUPS,)),
            dma((1,)),
            dma((GROUPS,)),
            dma((8, CHUNKS)),
            dma((8, CHUNKS)),
            dma((8, CHUNKS)),
            dma((8, CHUNKS)),
        ],
        compiler_params=pltpu.CompilerParams(
            collective_id=0, has_side_effects=True, vmem_limit_bytes=56 * 1024 * 1024
        ),
        cost_estimate=pl.CostEstimate(flops=8_500_000_000, bytes_accessed=11_500_000, transcendentals=200_000),
    )(tokens, routes.T, affinity.T, gate_proj, up_proj, down_proj)


def solution(mesh):
    in_specs = (
        P("group", "local"),
        P("group", None),
        P("group", None),
        P("group", None, "local"),
        P("group", None, "local"),
        P("group", None, "local"),
    )
    return jax.shard_map(
        on_device, mesh=mesh, in_specs=in_specs, out_specs=P("group", "local"), check_vma=False
    )
```

```python
import jax
import jax.numpy as jnp
from jax import lax
from jax.experimental import pallas as pl
from jax.experimental.pallas import tpu as pltpu
from jax.sharding import PartitionSpec as P

MESH = pl.DeviceIdType.MESH
F32, BF16 = jnp.float32, jnp.bfloat16

NY, NZ, NX = 4, 8, 4
GROUPS = NY * NZ
TOK, TOP, CAP = 64, 8, 24
FEAT, HPART = 896, 256
DEV = 2 * NX
ROWS = GROUPS * CAP
CHUNKS = NZ
CROWS = NY * CAP
HALF = CROWS // 2
DISTANCE = (1, 7, 4, 3, 5, 2, 6, 0)
AHEAD = 2

RIGHT, LEFT, RIGHT2, LEFT2, SIB_OWN, SIB_LEFT, SIB_RIGHT, SIB_FAR = range(8)


def distance_of(chunk):
    found = 0
    for index, value in enumerate(DISTANCE):
        if value:
            found = found + jnp.where(chunk == index, value, 0)
    return found


def kernel(
    tokens_ref, routes_ref, affinity_ref, gate_hbm, up_hbm, down_hbm, out_ref,
    gate_ref, up_ref, down_ref, outgoing, landed, rows, hidden, results, returned, weight_of, total,
    weight_sem, self_sem, sent_sem, landed_sem, back_sem, returned_sem, x_send, x_recv, h_send, h_recv,
):
    me_g, me_l = lax.axis_index("group"), lax.axis_index("local")
    y, z = me_g // NZ, lax.rem(me_g, NZ)
    x, core = me_l // 2, lax.rem(me_l, 2)
    right = lax.rem(x + 1, NX) * 2 + core
    left = lax.rem(x + NX - 1, NX) * 2 + core
    far = lax.rem(x + 2, NX) * 2 + core
    sibling = x * 2 + 1 - core

    def wrap(value, size):
        return jnp.where(value >= size, value - size, value)

    def group_at(dy, dz):
        return wrap(y + dy, NY) * NZ + wrap(z + dz, NZ)

    barrier = pltpu.get_barrier_semaphore()
    for offset in range(1, GROUPS):
        pl.semaphore_signal(
            barrier, inc=1, device_id=(wrap(me_g + offset, GROUPS), me_l), device_id_type=MESH
        )
    for peer in (right, left, sibling):
        pl.semaphore_signal(barrier, inc=1, device_id=(me_g, peer), device_id_type=MESH)

    weights = [
        pltpu.make_async_copy(source.at[0], target, weight_sem.at[index])
        for index, (source, target) in enumerate(
            ((gate_hbm, gate_ref), (up_hbm, up_ref), (down_hbm, down_ref))
        )
    ]
    for copy in weights:
        copy.start()

    block = lax.broadcasted_iota(jnp.int32, (GROUPS, TOK), 0)
    dz_of = distance_of(block // NY)
    dy_of = block - (block // NY) * NY
    yy, zz = y + NY - dy_of, z + NZ - dz_of
    yy = jnp.where(yy >= NY, yy - NY, yy)
    zz = jnp.where(zz >= NZ, zz - NZ, zz)
    expert = yy * NZ + zz
    named = jnp.zeros((GROUPS, TOK), F32)
    gates = jnp.zeros((GROUPS, TOK), F32)
    for k in range(TOP):
        same = routes_ref[k : k + 1, :] == expert
        named = named + jnp.where(same, 1.0, 0.0)
        gates = gates + jnp.where(same, affinity_ref[k : k + 1, :], 0.0)
    before = lax.broadcasted_iota(jnp.int32, (TOK, TOK), 0) < lax.broadcasted_iota(jnp.int32, (TOK, TOK), 1)
    earlier = jnp.dot(named.astype(BF16), jnp.where(before, 1.0, 0.0).astype(BF16), preferred_element_type=F32)
    slot = jnp.where(named > 0.5, earlier, -1.0).astype(jnp.int32)
    place = lax.broadcasted_iota(jnp.int32, (GROUPS, CAP, TOK), 1)
    holds = slot[:, None, :] == place
    pick = jnp.where(holds, 1.0, 0.0).reshape(ROWS, TOK).astype(BF16)
    for at in range(0, GROUPS, 8):
        part = jnp.dot(pick[at * CAP : (at + 8) * CAP], tokens_ref[...], preferred_element_type=F32)
        outgoing[at : at + 8] = part.reshape(8, CAP, FEAT).astype(BF16)

    pl.semaphore_wait(barrier, GROUPS - 1 + 3)

    own = DISTANCE.index(0) * NY
    own_chunk = own // NY
    self_copy = pltpu.make_async_copy(outgoing.at[own], landed.at[own], self_sem.at[0])
    self_copy.start()

    def dispatch(s, carry):
        dz, dy = distance_of(s // NY), lax.rem(s, NY)

        @pl.when(s != own)
        def _():
            pltpu.make_async_remote_copy(
                src_ref=outgoing.at[s],
                dst_ref=landed.at[s],
                send_sem=sent_sem.at[0],
                recv_sem=landed_sem.at[s],
                device_id=(group_at(NY - dy - jnp.where(dy == 0, NY, 0), NZ - dz - jnp.where(dz == 0, NZ, 0)), me_l),
                device_id_type=MESH,
            ).start()

        return carry

    lax.fori_loop(0, GROUPS, dispatch, 0)

    spread = jnp.where(holds, gates[:, None, :], 0.0).reshape(ROWS, TOK)
    high = spread.astype(BF16)
    low = (spread - high.astype(F32)).astype(BF16)
    weight_of[...] = jnp.concatenate([high.astype(F32), low.astype(F32)], axis=1).reshape(
        CHUNKS, CROWS, 2 * TOK
    )
    total[...] = jnp.zeros_like(total)

    def ring(buffer, send, recv, kind, chunk):
        start = pl.multiple_of(chunk * CROWS, CROWS)
        slot_of, begin, count, target = {
            RIGHT: (me_l, 0, CROWS, right),
            LEFT: (me_l, 0, CROWS, left),
            RIGHT2: (left, 0, HALF, right),
            LEFT2: (right, HALF, HALF, left),
            SIB_OWN: (me_l, 0, CROWS, sibling),
            SIB_LEFT: (left, 0, CROWS, sibling),
            SIB_RIGHT: (right, 0, CROWS, sibling),
            SIB_FAR: (far, 0, CROWS, sibling),
        }[kind]
        piece = buffer.at[slot_of, pl.ds(start + begin, count)]
        return pltpu.make_async_remote_copy(
            src_ref=piece,
            dst_ref=piece,
            send_sem=send.at[kind, chunk],
            recv_sem=recv.at[kind, chunk],
            device_id=(me_g, target),
            device_id_type=MESH,
        )

    def x_ring(kind, chunk):
        return ring(rows, x_send, x_recv, kind, chunk)

    def h_ring(kind, chunk):
        return ring(hidden, h_send, h_recv, kind, chunk)

    def begin_rows(chunk):
        for dy in range(NY):
            s = chunk * NY + dy

            @pl.when(s != own)
            def _():
                pltpu.make_async_copy(landed.at[s], landed.at[s], landed_sem.at[s]).wait()

            if dy == 0:

                @pl.when(s == own)
                def _():
                    self_copy.wait()

        blocks = landed[pl.ds(chunk * NY, NY)].astype(F32).reshape(CROWS, FEAT).astype(BF16)
        rows[me_l, pl.ds(pl.multiple_of(chunk * CROWS, CROWS), CROWS)] = blocks
        for kind in (RIGHT, LEFT, SIB_OWN):
            x_ring(kind, chunk).start()

    def second(make, chunk):
        make(RIGHT, chunk).wait_recv()
        make(RIGHT2, chunk).start()
        make(SIB_LEFT, chunk).start()
        make(LEFT, chunk).wait_recv()
        make(LEFT2, chunk).start()
        make(SIB_RIGHT, chunk).start()

    def third(make, chunk):
        make(RIGHT2, chunk).wait_recv()
        make(LEFT2, chunk).wait_recv()
        make(SIB_FAR, chunk).start()

    def gathered(make, chunk):
        for kind in (SIB_OWN, SIB_LEFT, SIB_RIGHT, SIB_FAR):
            make(kind, chunk).wait_recv()

    def hidden_rows(chunk):
        here = pl.ds(pl.multiple_of(chunk * CROWS, CROWS), CROWS)
        gate = jnp.zeros((CROWS, HPART), F32)
        up = jnp.zeros((CROWS, HPART), F32)
        for pair in range(NX):
            lhs = jnp.concatenate([rows[2 * pair, here], rows[2 * pair + 1, here]], axis=1)
            depth = slice(pair * 2 * FEAT, (pair + 1) * 2 * FEAT)
            gate = gate + jnp.dot(lhs, gate_ref[depth, :], preferred_element_type=F32)
            up = up + jnp.dot(lhs, up_ref[depth, :], preferred_element_type=F32)
        value = gate / (1.0 + jnp.exp(-gate)) * up
        hidden[me_l, here] = value.astype(BF16)

    def output_rows(chunk):
        here = pl.ds(pl.multiple_of(chunk * CROWS, CROWS), CROWS)
        lhs = jnp.concatenate([hidden[part, here] for part in range(DEV)], axis=1)
        value = jnp.dot(lhs, down_ref[...], preferred_element_type=F32)
        results[pl.ds(chunk * NY, NY)] = value.reshape(NY, CAP, FEAT).astype(BF16)

    def send_back(chunk):
        dz = distance_of(chunk)
        for dy in range(NY):
            s = chunk * NY + dy

            @pl.when(s != own)
            def _():
                pltpu.make_async_remote_copy(
                    src_ref=results.at[s],
                    dst_ref=returned.at[s],
                    send_sem=back_sem.at[0],
                    recv_sem=returned_sem.at[s],
                    device_id=(group_at(dy, dz), me_l),
                    device_id_type=MESH,
                ).start()

            if dy == 0:

                @pl.when(s == own)
                def _():
                    pltpu.make_async_copy(results.at[s], returned.at[s], self_sem.at[1]).start()

    def combine(chunk):
        for dy in range(NY):
            s = chunk * NY + dy

            @pl.when(s != own)
            def _():
                pltpu.make_async_copy(returned.at[s], returned.at[s], returned_sem.at[s]).wait()

            if dy == 0:

                @pl.when(s == own)
                def _():
                    pltpu.make_async_copy(results.at[s], returned.at[s], self_sem.at[1]).wait()

        values = returned[pl.ds(chunk * NY, NY)].astype(F32).reshape(CROWS, FEAT).astype(BF16)
        both = lax.dot_general(
            weight_of[chunk].astype(BF16), values, (((0,), (0,)), ((), ())), preferred_element_type=F32
        )
        total[...] += both[:TOK] + both[TOK:]

    def early(chunk, carry):
        begin_rows(chunk)
        return carry

    lax.fori_loop(0, AHEAD, early, 0)

    def turn(i, carry):
        @pl.when(i < CHUNKS)
        def _():
            second(x_ring, i)

        @pl.when(i + AHEAD < CHUNKS)
        def _():
            begin_rows(i + AHEAD)

        @pl.when((i >= 1) & (i < CHUNKS + 1))
        def _():
            third(x_ring, i - 1)

        @pl.when((i >= 2) & (i < CHUNKS + 2))
        def _():
            second(h_ring, i - 2)

        @pl.when(i >= 3)
        def _():
            third(h_ring, i - 3)

        @pl.when(i == 1)
        def _():
            weights[0].wait()
            weights[1].wait()

        @pl.when((i >= 1) & (i < CHUNKS + 1))
        def _():
            gathered(x_ring, i - 1)
            hidden_rows(i - 1)
            for kind in (RIGHT, LEFT, SIB_OWN):
                h_ring(kind, i - 1).start()

        @pl.when(i == 3)
        def _():
            weights[2].wait()

        @pl.when(i >= 3)
        def _():
            gathered(h_ring, i - 3)
            output_rows(i - 3)
            send_back(i - 3)

        return carry

    lax.fori_loop(0, CHUNKS + 3, turn, 0)

    def collect(chunk, carry):
        combine(chunk)
        return carry

    lax.fori_loop(0, CHUNKS, collect, 0)
    out_ref[...] = total[...].astype(BF16)

    def settle(chunk, carry):
        for kind in range(8):
            x_ring(kind, chunk).wait_send()
            h_ring(kind, chunk).wait_send()
        return carry

    lax.fori_loop(0, CHUNKS, settle, 0)
    others = pl.ds(0, GROUPS - 1)
    pltpu.make_async_copy(outgoing.at[others], outgoing.at[others], sent_sem.at[0]).wait()
    pltpu.make_async_copy(results.at[others], results.at[others], back_sem.at[0]).wait()


def on_device(tokens, routes, affinity, gate_proj, up_proj, down_proj):
    vmem, anywhere = pl.BlockSpec(memory_space=pltpu.VMEM), pl.BlockSpec(memory_space=pl.ANY)
    dma = pltpu.SemaphoreType.DMA
    return pl.pallas_call(
        kernel,
        out_shape=jax.ShapeDtypeStruct((TOK, FEAT), BF16),
        in_specs=[vmem, vmem, vmem, anywhere, anywhere, anywhere],
        out_specs=vmem,
        scratch_shapes=[
            pltpu.VMEM((DEV * FEAT, HPART), BF16),
            pltpu.VMEM((DEV * FEAT, HPART), BF16),
            pltpu.VMEM((DEV * HPART, FEAT), BF16),
            pltpu.VMEM((GROUPS, CAP, FEAT), BF16),
            pltpu.VMEM((GROUPS, CAP, FEAT), BF16),
            pltpu.VMEM((DEV, ROWS, FEAT), BF16),
            pltpu.VMEM((DEV, ROWS, HPART), BF16),
            pltpu.VMEM((GROUPS, CAP, FEAT), BF16),
            pltpu.VMEM((GROUPS, CAP, FEAT), BF16),
            pltpu.VMEM((CHUNKS, CROWS, 2 * TOK), F32),
            pltpu.VMEM((TOK, FEAT), F32),
            dma((3,)),
            dma((2,)),
            dma((1,)),
            dma((GROUPS,)),
            dma((1,)),
            dma((GROUPS,)),
            dma((8, CHUNKS)),
            dma((8, CHUNKS)),
            dma((8, CHUNKS)),
            dma((8, CHUNKS)),
        ],
        compiler_params=pltpu.CompilerParams(
            collective_id=0, has_side_effects=True, vmem_limit_bytes=56 * 1024 * 1024
        ),
        cost_estimate=pl.CostEstimate(flops=8_500_000_000, bytes_accessed=11_500_000, transcendentals=200_000),
    )(tokens, routes.T, affinity.T, gate_proj, up_proj, down_proj)


def solution(mesh):
    in_specs = (
        P("group", "local"),
        P("group", None),
        P("group", None),
        P("group", None, "local"),
        P("group", None, "local"),
        P("group", None, "local"),
    )
    return jax.shard_map(
        on_device, mesh=mesh, in_specs=in_specs, out_specs=P("group", "local"), check_vma=False
    )
```

```python
import jax
import jax.numpy as jnp
from jax import lax
from jax.experimental import pallas as pl
from jax.experimental.pallas import tpu as pltpu
from jax.sharding import PartitionSpec as P

MESH = pl.DeviceIdType.MESH
F32, BF16 = jnp.float32, jnp.bfloat16

NY, NZ, NX = 4, 8, 4
GROUPS = NY * NZ
TOK, TOP, CAP = 64, 8, 24
FEAT, HPART = 896, 256
DEV = 2 * NX
ROWS = GROUPS * CAP
CHUNKS = NZ
CROWS = NY * CAP
HALF = CROWS // 2
DISTANCE = (1, 7, 4, 3, 5, 2, 6, 0)
AHEAD = 2

RIGHT, LEFT, RIGHT2, LEFT2, SIBLING = range(5)
FAR = RIGHT2


def distance_of(chunk):
    found = 0
    for index, value in enumerate(DISTANCE):
        if value:
            found = found + jnp.where(chunk == index, value, 0)
    return found


def kernel(
    tokens_ref, routes_ref, affinity_ref, gate_hbm, up_hbm, down_hbm, out_ref,
    gate_ref, up_ref, down_ref, outgoing, landed, rows, hidden, results, returned, weight_of, total,
    weight_sem, sent_sem, landed_sem, back_sem, returned_sem, x_send, x_recv, h_send, h_recv,
):
    me_g, me_l = lax.axis_index("group"), lax.axis_index("local")
    y, z = me_g // NZ, lax.rem(me_g, NZ)
    x, core = me_l // 2, lax.rem(me_l, 2)
    right = lax.rem(x + 1, NX) * 2 + core
    left = lax.rem(x + NX - 1, NX) * 2 + core
    right_x, left_x, far_x = lax.rem(x + 1, NX), lax.rem(x + NX - 1, NX), lax.rem(x + 2, NX)
    sibling = x * 2 + 1 - core

    def wrap(value, size):
        return jnp.where(value >= size, value - size, value)

    def group_at(dy, dz):
        return wrap(y + dy, NY) * NZ + wrap(z + dz, NZ)

    barrier = pltpu.get_barrier_semaphore()
    for offset in range(1, GROUPS):
        pl.semaphore_signal(
            barrier, inc=1, device_id=(wrap(me_g + offset, GROUPS), me_l), device_id_type=MESH
        )
    for peer in (right, left, sibling):
        pl.semaphore_signal(barrier, inc=1, device_id=(me_g, peer), device_id_type=MESH)

    weights = [
        pltpu.make_async_copy(source.at[0], target, weight_sem.at[index])
        for index, (source, target) in enumerate(
            ((gate_hbm, gate_ref), (up_hbm, up_ref), (down_hbm, down_ref))
        )
    ]
    for copy in weights:
        copy.start()

    block = lax.broadcasted_iota(jnp.int32, (GROUPS, TOK), 0)
    dz_of = distance_of(block // NY)
    dy_of = block - (block // NY) * NY
    yy, zz = y + NY - dy_of, z + NZ - dz_of
    yy = jnp.where(yy >= NY, yy - NY, yy)
    zz = jnp.where(zz >= NZ, zz - NZ, zz)
    expert = yy * NZ + zz
    named = jnp.zeros((GROUPS, TOK), F32)
    gates = jnp.zeros((GROUPS, TOK), F32)
    for k in range(TOP):
        same = routes_ref[k : k + 1, :] == expert
        named = named + jnp.where(same, 1.0, 0.0)
        gates = gates + jnp.where(same, affinity_ref[k : k + 1, :], 0.0)
    before = lax.broadcasted_iota(jnp.int32, (TOK, TOK), 0) < lax.broadcasted_iota(jnp.int32, (TOK, TOK), 1)
    earlier = jnp.dot(named.astype(BF16), jnp.where(before, 1.0, 0.0).astype(BF16), preferred_element_type=F32)
    slot = jnp.where(named > 0.5, earlier, -1.0).astype(jnp.int32)
    place = lax.broadcasted_iota(jnp.int32, (GROUPS, CAP, TOK), 1)
    holds = slot[:, None, :] == place
    pick = jnp.where(holds, 1.0, 0.0).reshape(ROWS, TOK).astype(BF16)
    for at in range(0, GROUPS, 8):
        part = jnp.dot(pick[at * CAP : (at + 8) * CAP], tokens_ref[...], preferred_element_type=F32)
        outgoing[at : at + 8] = part.reshape(8, CAP, FEAT).astype(BF16)

    pl.semaphore_wait(barrier, GROUPS - 1 + 3)

    own = DISTANCE.index(0) * NY
    pltpu.make_async_copy(outgoing.at[own], landed.at[own], landed_sem.at[own // NY]).start()

    def dispatch(s, carry):
        dz, dy = distance_of(s // NY), lax.rem(s, NY)

        @pl.when(s != own)
        def _():
            pltpu.make_async_remote_copy(
                src_ref=outgoing.at[s],
                dst_ref=landed.at[s],
                send_sem=sent_sem.at[0],
                recv_sem=landed_sem.at[s // NY],
                device_id=(group_at(NY - dy - jnp.where(dy == 0, NY, 0), NZ - dz - jnp.where(dz == 0, NZ, 0)), me_l),
                device_id_type=MESH,
            ).start()

        return carry

    lax.fori_loop(0, GROUPS, dispatch, 0)

    spread = jnp.where(holds, gates[:, None, :], 0.0).reshape(ROWS, TOK)
    high = spread.astype(BF16)
    low = (spread - high.astype(F32)).astype(BF16)
    weight_of[...] = jnp.concatenate([high.astype(F32), low.astype(F32)], axis=1).reshape(
        CHUNKS, CROWS, 2 * TOK
    )
    total[...] = jnp.zeros_like(total)

    def ring(buffer, send, recv, kind, chunk):
        start = pl.multiple_of(chunk * CROWS, CROWS)
        slots, begin, count, target = {
            RIGHT: (x, 0, CROWS, right),
            LEFT: (x, 0, CROWS, left),
            RIGHT2: (left_x, 0, HALF, right),
            LEFT2: (right_x, HALF, HALF, left),
            SIBLING: (pl.ds(0, NX), 0, CROWS, sibling),
        }[kind]
        piece = buffer.at[core, slots, pl.ds(start + begin, count)]
        return pltpu.make_async_remote_copy(
            src_ref=piece,
            dst_ref=piece,
            send_sem=send.at[kind],
            recv_sem=recv.at[FAR if kind == LEFT2 else kind, chunk],
            device_id=(me_g, target),
            device_id_type=MESH,
        )

    def arrival(buffer, recv, kind, chunk):
        here = pl.ds(pl.multiple_of(chunk * CROWS, CROWS), CROWS)
        piece = {
            RIGHT: lambda: buffer.at[core, left_x, here],
            LEFT: lambda: buffer.at[core, right_x, here],
            FAR: lambda: buffer.at[core, far_x, here],
            SIBLING: lambda: buffer.at[1 - core, pl.ds(0, NX), here],
        }[kind]()
        pltpu.make_async_copy(piece, piece, recv.at[kind, chunk]).wait()

    x_ring, h_ring = (rows, x_send, x_recv), (hidden, h_send, h_recv)

    def begin_rows(chunk):
        blocks_of = landed.at[pl.ds(chunk * NY, NY)]
        pltpu.make_async_copy(blocks_of, blocks_of, landed_sem.at[chunk]).wait()
        blocks = blocks_of[...].astype(F32).reshape(CROWS, FEAT).astype(BF16)
        rows[core, x, pl.ds(pl.multiple_of(chunk * CROWS, CROWS), CROWS)] = blocks
        for kind in (RIGHT, LEFT):
            ring(*x_ring, kind, chunk).start()

    def second(kit, chunk):
        for kind, onward in ((RIGHT, RIGHT2), (LEFT, LEFT2)):
            arrival(kit[0], kit[2], kind, chunk)
            ring(*kit, onward, chunk).start()

    def third(kit, chunk):
        arrival(kit[0], kit[2], FAR, chunk)
        ring(*kit, SIBLING, chunk).start()

    def gathered(kit, chunk):
        arrival(kit[0], kit[2], SIBLING, chunk)

    def hidden_rows(chunk):
        here = pl.ds(pl.multiple_of(chunk * CROWS, CROWS), CROWS)
        gate = jnp.zeros((CROWS, HPART), F32)
        up = jnp.zeros((CROWS, HPART), F32)
        for pair in range(NX):
            lhs = jnp.concatenate([rows[0, pair, here], rows[1, pair, here]], axis=1)
            depth = slice(pair * 2 * FEAT, (pair + 1) * 2 * FEAT)
            gate = gate + jnp.dot(lhs, gate_ref[depth, :], preferred_element_type=F32)
            up = up + jnp.dot(lhs, up_ref[depth, :], preferred_element_type=F32)
        value = gate / (1.0 + jnp.exp(-gate)) * up
        hidden[core, x, here] = value.astype(BF16)

    def output_rows(chunk):
        here = pl.ds(pl.multiple_of(chunk * CROWS, CROWS), CROWS)
        lhs = jnp.concatenate([hidden[part % 2, part // 2, here] for part in range(DEV)], axis=1)
        value = jnp.dot(lhs, down_ref[...], preferred_element_type=F32)
        results[pl.ds(chunk * NY, NY)] = value.reshape(NY, CAP, FEAT).astype(BF16)

    def send_back(chunk):
        dz = distance_of(chunk)
        for dy in range(NY):
            s = chunk * NY + dy

            @pl.when(s != own)
            def _():
                pltpu.make_async_remote_copy(
                    src_ref=results.at[s],
                    dst_ref=returned.at[s],
                    send_sem=back_sem.at[0],
                    recv_sem=returned_sem.at[chunk],
                    device_id=(group_at(dy, dz), me_l),
                    device_id_type=MESH,
                ).start()

            if dy == 0:

                @pl.when(s == own)
                def _():
                    pltpu.make_async_copy(results.at[s], returned.at[s], returned_sem.at[chunk]).start()

    def combine(chunk):
        blocks_of = returned.at[pl.ds(chunk * NY, NY)]
        pltpu.make_async_copy(blocks_of, blocks_of, returned_sem.at[chunk]).wait()
        values = blocks_of[...].astype(F32).reshape(CROWS, FEAT).astype(BF16)
        both = lax.dot_general(
            weight_of[chunk].astype(BF16), values, (((0,), (0,)), ((), ())), preferred_element_type=F32
        )
        total[...] += both[:TOK] + both[TOK:]

    def early(chunk, carry):
        begin_rows(chunk)
        return carry

    lax.fori_loop(0, AHEAD, early, 0)

    def turn(i, carry):
        @pl.when((i >= 1) & (i < CHUNKS + 1))
        def _():
            third(x_ring, i - 1)

        @pl.when(i >= 3)
        def _():
            third(h_ring, i - 3)

        @pl.when(i < CHUNKS)
        def _():
            second(x_ring, i)

        @pl.when(i + AHEAD < CHUNKS)
        def _():
            begin_rows(i + AHEAD)

        @pl.when(i == 3)
        def _():
            weights[2].wait()

        @pl.when(i >= 3)
        def _():
            gathered(h_ring, i - 3)
            output_rows(i - 3)
            send_back(i - 3)

        @pl.when((i >= 2) & (i < CHUNKS + 2))
        def _():
            second(h_ring, i - 2)

        @pl.when(i == 1)
        def _():
            weights[0].wait()
            weights[1].wait()

        @pl.when((i >= 1) & (i < CHUNKS + 1))
        def _():
            gathered(x_ring, i - 1)
            hidden_rows(i - 1)
            for kind in (RIGHT, LEFT):
                ring(*h_ring, kind, i - 1).start()

        return carry

    lax.fori_loop(0, CHUNKS + 3, turn, 0)

    def collect(chunk, carry):
        combine(chunk)
        return carry

    lax.fori_loop(0, CHUNKS, collect, 0)
    out_ref[...] = total[...].astype(BF16)

    for buffer, send, _ in (x_ring, h_ring):
        for kind, piece in (
            (RIGHT, buffer.at[core, x]),
            (LEFT, buffer.at[core, x]),
            (RIGHT2, buffer.at[core, left_x, pl.ds(0, ROWS // 2)]),
            (LEFT2, buffer.at[core, right_x, pl.ds(0, ROWS // 2)]),
            (SIBLING, buffer.at[core]),
        ):
            pltpu.make_async_copy(piece, piece, send.at[kind]).wait()
    others = pl.ds(0, GROUPS - 1)
    pltpu.make_async_copy(outgoing.at[others], outgoing.at[others], sent_sem.at[0]).wait()
    pltpu.make_async_copy(results.at[others], results.at[others], back_sem.at[0]).wait()


def on_device(tokens, routes, affinity, gate_proj, up_proj, down_proj):
    vmem, anywhere = pl.BlockSpec(memory_space=pltpu.VMEM), pl.BlockSpec(memory_space=pl.ANY)
    dma = pltpu.SemaphoreType.DMA
    return pl.pallas_call(
        kernel,
        out_shape=pltpu.VMEM((TOK, FEAT), BF16),
        in_specs=[vmem, vmem, vmem, anywhere, anywhere, anywhere],
        out_specs=vmem,
        scratch_shapes=[
            pltpu.VMEM((DEV * FEAT, HPART), BF16),
            pltpu.VMEM((DEV * FEAT, HPART), BF16),
            pltpu.VMEM((DEV * HPART, FEAT), BF16),
            pltpu.VMEM((GROUPS, CAP, FEAT), BF16),
            pltpu.VMEM((GROUPS, CAP, FEAT), BF16),
            pltpu.VMEM((2, NX, ROWS, FEAT), BF16),
            pltpu.VMEM((2, NX, ROWS, HPART), BF16),
            pltpu.VMEM((GROUPS, CAP, FEAT), BF16),
            pltpu.VMEM((GROUPS, CAP, FEAT), BF16),
            pltpu.VMEM((CHUNKS, CROWS, 2 * TOK), F32),
            pltpu.VMEM((TOK, FEAT), F32),
            dma((3,)),
            dma((1,)),
            dma((CHUNKS,)),
            dma((1,)),
            dma((CHUNKS,)),
            dma((5,)),
            dma((5, CHUNKS)),
            dma((5,)),
            dma((5, CHUNKS)),
        ],
        compiler_params=pltpu.CompilerParams(
            collective_id=0, has_side_effects=True, vmem_limit_bytes=56 * 1024 * 1024
        ),
        cost_estimate=pl.CostEstimate(flops=8_500_000_000, bytes_accessed=11_500_000, transcendentals=200_000),
    )(tokens, routes.T, affinity.T, gate_proj, up_proj, down_proj)


def solution(mesh):
    in_specs = (
        P("group", "local"),
        P("group", None),
        P("group", None),
        P("group", None, "local"),
        P("group", None, "local"),
        P("group", None, "local"),
    )
    return jax.shard_map(
        on_device, mesh=mesh, in_specs=in_specs, out_specs=P("group", "local"), check_vma=False
    )
```

```python
import jax
import jax.numpy as jnp
from jax import lax
from jax.experimental import pallas as pl
from jax.experimental.pallas import tpu as pltpu
from jax.sharding import PartitionSpec as P

MESH = pl.DeviceIdType.MESH
F32, BF16 = jnp.float32, jnp.bfloat16

NY, NZ, NX = 4, 8, 4
GROUPS = NY * NZ
TOK, TOP, CAP = 64, 8, 24
FEAT, HPART = 896, 256
DEV = 2 * NX
ROWS = GROUPS * CAP
CHUNKS = NZ
CROWS = NY * CAP
HALF = CROWS // 2
DISTANCE = (1, 7, 2, 6, 3, 5, 4, 0)
AHEAD = 2

RIGHT, LEFT, RIGHT2, LEFT2, SIBLING, OVER = range(6)
FAR = RIGHT2


def distance_of(chunk):
    found = 0
    for index, value in enumerate(DISTANCE):
        if value:
            found = found + jnp.where(chunk == index, value, 0)
    return found


def kernel(
    tokens_ref, routes_ref, affinity_ref, gate_hbm, up_hbm, down_hbm, out_ref,
    gate_ref, up_ref, down_ref, outgoing, landed, rows, hidden, results, returned, weight_of, total,
    weight_sem, sent_sem, landed_sem, back_sem, returned_sem, x_send, x_recv, h_send, h_recv,
):
    me_g, me_l = lax.axis_index("group"), lax.axis_index("local")
    y, z = me_g // NZ, lax.rem(me_g, NZ)
    x, core = me_l // 2, lax.rem(me_l, 2)
    right = lax.rem(x + 1, NX) * 2 + core
    left = lax.rem(x + NX - 1, NX) * 2 + core
    far = lax.rem(x + 2, NX) * 2 + core
    right_x, left_x, far_x = lax.rem(x + 1, NX), lax.rem(x + NX - 1, NX), lax.rem(x + 2, NX)
    sibling = x * 2 + 1 - core

    def wrap(value, size):
        return jnp.where(value >= size, value - size, value)

    def group_at(dy, dz):
        return wrap(y + dy, NY) * NZ + wrap(z + dz, NZ)

    barrier = pltpu.get_barrier_semaphore()
    for offset in range(1, GROUPS):
        pl.semaphore_signal(
            barrier, inc=1, device_id=(wrap(me_g + offset, GROUPS), me_l), device_id_type=MESH
        )
    for peer in (right, left, far, sibling):
        pl.semaphore_signal(barrier, inc=1, device_id=(me_g, peer), device_id_type=MESH)

    weights = [
        pltpu.make_async_copy(source.at[0], target, weight_sem.at[index])
        for index, (source, target) in enumerate(
            ((gate_hbm, gate_ref), (up_hbm, up_ref), (down_hbm, down_ref))
        )
    ]
    for copy in weights:
        copy.start()

    block = lax.broadcasted_iota(jnp.int32, (GROUPS, TOK), 0)
    dz_of = distance_of(block // NY)
    dy_of = block - (block // NY) * NY
    yy, zz = y + NY - dy_of, z + NZ - dz_of
    yy = jnp.where(yy >= NY, yy - NY, yy)
    zz = jnp.where(zz >= NZ, zz - NZ, zz)
    expert = yy * NZ + zz
    named = jnp.zeros((GROUPS, TOK), F32)
    gates = jnp.zeros((GROUPS, TOK), F32)
    for k in range(TOP):
        same = routes_ref[k : k + 1, :] == expert
        named = named + jnp.where(same, 1.0, 0.0)
        gates = gates + jnp.where(same, affinity_ref[k : k + 1, :], 0.0)
    before = lax.broadcasted_iota(jnp.int32, (TOK, TOK), 0) < lax.broadcasted_iota(jnp.int32, (TOK, TOK), 1)
    earlier = jnp.dot(named.astype(BF16), jnp.where(before, 1.0, 0.0).astype(BF16), preferred_element_type=F32)
    slot = jnp.where(named > 0.5, earlier, -1.0).astype(jnp.int32)
    place = lax.broadcasted_iota(jnp.int32, (GROUPS, CAP, TOK), 1)
    holds = slot[:, None, :] == place
    pick = jnp.where(holds, 1.0, 0.0).reshape(ROWS, TOK).astype(BF16)
    for at in range(0, GROUPS, 8):
        part = jnp.dot(pick[at * CAP : (at + 8) * CAP], tokens_ref[...], preferred_element_type=F32)
        outgoing[at : at + 8] = part.reshape(8, CAP, FEAT).astype(BF16)

    pl.semaphore_wait(barrier, GROUPS - 1 + 4)

    own = DISTANCE.index(0) * NY
    pltpu.make_async_copy(outgoing.at[own], landed.at[own], landed_sem.at[own // NY]).start()

    def dispatch(s, carry):
        dz, dy = distance_of(s // NY), lax.rem(s, NY)

        @pl.when(s != own)
        def _():
            pltpu.make_async_remote_copy(
                src_ref=outgoing.at[s],
                dst_ref=landed.at[s],
                send_sem=sent_sem.at[0],
                recv_sem=landed_sem.at[s // NY],
                device_id=(group_at(NY - dy - jnp.where(dy == 0, NY, 0), NZ - dz - jnp.where(dz == 0, NZ, 0)), me_l),
                device_id_type=MESH,
            ).start()

        return carry

    lax.fori_loop(0, GROUPS, dispatch, 0)

    spread = jnp.where(holds, gates[:, None, :], 0.0).reshape(ROWS, TOK)
    high = spread.astype(BF16)
    low = (spread - high.astype(F32)).astype(BF16)
    weight_of[...] = jnp.concatenate([high.astype(F32), low.astype(F32)], axis=1).reshape(
        CHUNKS, CROWS, 2 * TOK
    )
    total[...] = jnp.zeros_like(total)

    def ring(buffer, send, recv, kind, chunk):
        start = pl.multiple_of(chunk * CROWS, CROWS)
        slots, begin, count, target = {
            RIGHT: (x, 0, CROWS, right),
            LEFT: (x, 0, CROWS, left),
            RIGHT2: (left_x, 0, HALF, right),
            LEFT2: (right_x, HALF, HALF, left),
            SIBLING: (pl.ds(0, NX), 0, CROWS, sibling),
            OVER: (x, 0, CROWS, far),
        }[kind]
        piece = buffer.at[core, slots, pl.ds(start + begin, count)]
        return pltpu.make_async_remote_copy(
            src_ref=piece,
            dst_ref=piece,
            send_sem=send.at[kind],
            recv_sem=recv.at[FAR if kind in (LEFT2, OVER) else kind, chunk],
            device_id=(me_g, target),
            device_id_type=MESH,
        )

    def arrival(buffer, recv, kind, chunk):
        here = pl.ds(pl.multiple_of(chunk * CROWS, CROWS), CROWS)
        piece = {
            RIGHT: lambda: buffer.at[core, left_x, here],
            LEFT: lambda: buffer.at[core, right_x, here],
            FAR: lambda: buffer.at[core, far_x, here],
            SIBLING: lambda: buffer.at[1 - core, pl.ds(0, NX), here],
        }[kind]()
        pltpu.make_async_copy(piece, piece, recv.at[kind, chunk]).wait()

    x_ring, h_ring = (rows, x_send, x_recv), (hidden, h_send, h_recv)

    def begin_rows(chunk):
        blocks_of = landed.at[pl.ds(chunk * NY, NY)]
        pltpu.make_async_copy(blocks_of, blocks_of, landed_sem.at[chunk]).wait()
        blocks = blocks_of[...].astype(F32).reshape(CROWS, FEAT).astype(BF16)
        rows[core, x, pl.ds(pl.multiple_of(chunk * CROWS, CROWS), CROWS)] = blocks
        for kind in (RIGHT, LEFT):
            ring(*x_ring, kind, chunk).start()

    def second(kit, chunk):
        for kind, onward in ((RIGHT, RIGHT2), (LEFT, LEFT2)):
            arrival(kit[0], kit[2], kind, chunk)
            ring(*kit, onward, chunk).start()

    def third(kit, chunk):
        arrival(kit[0], kit[2], FAR, chunk)
        ring(*kit, SIBLING, chunk).start()

    def all_over(kit, chunk):
        for kind in (RIGHT, LEFT, FAR):
            arrival(kit[0], kit[2], kind, chunk)
        ring(*kit, SIBLING, chunk).start()

    def gathered(kit, chunk):
        arrival(kit[0], kit[2], SIBLING, chunk)

    def hidden_rows(chunk):
        here = pl.ds(pl.multiple_of(chunk * CROWS, CROWS), CROWS)
        gate = jnp.zeros((CROWS, HPART), F32)
        up = jnp.zeros((CROWS, HPART), F32)
        for pair in range(NX):
            lhs = jnp.concatenate([rows[0, pair, here], rows[1, pair, here]], axis=1)
            depth = slice(pair * 2 * FEAT, (pair + 1) * 2 * FEAT)
            gate = gate + jnp.dot(lhs, gate_ref[depth, :], preferred_element_type=F32)
            up = up + jnp.dot(lhs, up_ref[depth, :], preferred_element_type=F32)
        value = gate / (1.0 + jnp.exp(-gate)) * up
        hidden[core, x, here] = value.astype(BF16)

    def output_rows(chunk):
        here = pl.ds(pl.multiple_of(chunk * CROWS, CROWS), CROWS)
        lhs = jnp.concatenate([hidden[part % 2, part // 2, here] for part in range(DEV)], axis=1)
        value = jnp.dot(lhs, down_ref[...], preferred_element_type=F32)
        results[pl.ds(chunk * NY, NY)] = value.reshape(NY, CAP, FEAT).astype(BF16)

    def send_back(chunk):
        dz = distance_of(chunk)
        for dy in range(NY):
            s = chunk * NY + dy

            @pl.when(s != own)
            def _():
                pltpu.make_async_remote_copy(
                    src_ref=results.at[s],
                    dst_ref=returned.at[s],
                    send_sem=back_sem.at[0],
                    recv_sem=returned_sem.at[chunk],
                    device_id=(group_at(dy, dz), me_l),
                    device_id_type=MESH,
                ).start()

            if dy == 0:

                @pl.when(s == own)
                def _():
                    pltpu.make_async_copy(results.at[s], returned.at[s], returned_sem.at[chunk]).start()

    def combine(chunk):
        blocks_of = returned.at[pl.ds(chunk * NY, NY)]
        pltpu.make_async_copy(blocks_of, blocks_of, returned_sem.at[chunk]).wait()
        values = blocks_of[...].astype(F32).reshape(CROWS, FEAT).astype(BF16)
        both = lax.dot_general(
            weight_of[chunk].astype(BF16), values, (((0,), (0,)), ((), ())), preferred_element_type=F32
        )
        total[...] += both[:TOK] + both[TOK:]

    def early(chunk, carry):
        begin_rows(chunk)
        return carry

    lax.fori_loop(0, AHEAD, early, 0)

    def turn(i, carry):
        @pl.when((i >= 1) & (i < CHUNKS + 1))
        def _():
            third(x_ring, i - 1)

        @pl.when(i < CHUNKS)
        def _():
            second(x_ring, i)

        @pl.when(i >= 2)
        def _():
            all_over(h_ring, i - 2)

        @pl.when(i == 1)
        def _():
            weights[0].wait()
            weights[1].wait()

        @pl.when((i >= 1) & (i < CHUNKS + 1))
        def _():
            gathered(x_ring, i - 1)
            hidden_rows(i - 1)
            for kind in (RIGHT, LEFT, OVER):
                ring(*h_ring, kind, i - 1).start()

        @pl.when(i + AHEAD < CHUNKS)
        def _():
            begin_rows(i + AHEAD)

        @pl.when(i == 2)
        def _():
            weights[2].wait()

        @pl.when(i >= 2)
        def _():
            gathered(h_ring, i - 2)
            output_rows(i - 2)
            send_back(i - 2)

        return carry

    lax.fori_loop(0, CHUNKS + 2, turn, 0)

    def collect(chunk, carry):
        combine(chunk)
        return carry

    lax.fori_loop(0, CHUNKS, collect, 0)
    out_ref[...] = total[...].astype(BF16)

    half = pl.ds(0, ROWS // 2)
    for send, kind, piece in (
        (x_send, RIGHT, rows.at[core, x]),
        (x_send, LEFT, rows.at[core, x]),
        (x_send, RIGHT2, rows.at[core, left_x, half]),
        (x_send, LEFT2, rows.at[core, right_x, half]),
        (x_send, SIBLING, rows.at[core]),
        (h_send, RIGHT, hidden.at[core, x]),
        (h_send, LEFT, hidden.at[core, x]),
        (h_send, OVER, hidden.at[core, x]),
        (h_send, SIBLING, hidden.at[core]),
    ):
        pltpu.make_async_copy(piece, piece, send.at[kind]).wait()
    others = pl.ds(0, GROUPS - 1)
    pltpu.make_async_copy(outgoing.at[others], outgoing.at[others], sent_sem.at[0]).wait()
    pltpu.make_async_copy(results.at[others], results.at[others], back_sem.at[0]).wait()


def on_device(tokens, routes, affinity, gate_proj, up_proj, down_proj):
    vmem, anywhere = pl.BlockSpec(memory_space=pltpu.VMEM), pl.BlockSpec(memory_space=pl.ANY)
    dma = pltpu.SemaphoreType.DMA
    return pl.pallas_call(
        kernel,
        out_shape=pltpu.VMEM((TOK, FEAT), BF16),
        in_specs=[vmem, vmem, vmem, anywhere, anywhere, anywhere],
        out_specs=vmem,
        scratch_shapes=[
            pltpu.VMEM((DEV * FEAT, HPART), BF16),
            pltpu.VMEM((DEV * FEAT, HPART), BF16),
            pltpu.VMEM((DEV * HPART, FEAT), BF16),
            pltpu.VMEM((GROUPS, CAP, FEAT), BF16),
            pltpu.VMEM((GROUPS, CAP, FEAT), BF16),
            pltpu.VMEM((2, NX, ROWS, FEAT), BF16),
            pltpu.VMEM((2, NX, ROWS, HPART), BF16),
            pltpu.VMEM((GROUPS, CAP, FEAT), BF16),
            pltpu.VMEM((GROUPS, CAP, FEAT), BF16),
            pltpu.VMEM((CHUNKS, CROWS, 2 * TOK), F32),
            pltpu.VMEM((TOK, FEAT), F32),
            dma((3,)),
            dma((1,)),
            dma((CHUNKS,)),
            dma((1,)),
            dma((CHUNKS,)),
            dma((6,)),
            dma((6, CHUNKS)),
            dma((6,)),
            dma((6, CHUNKS)),
        ],
        compiler_params=pltpu.CompilerParams(
            collective_id=0, has_side_effects=True, vmem_limit_bytes=56 * 1024 * 1024
        ),
        cost_estimate=pl.CostEstimate(flops=8_500_000_000, bytes_accessed=11_500_000, transcendentals=200_000),
    )(tokens, routes.T, affinity.T, gate_proj, up_proj, down_proj)


def solution(mesh):
    in_specs = (
        P("group", "local"),
        P("group", None),
        P("group", None),
        P("group", None, "local"),
        P("group", None, "local"),
        P("group", None, "local"),
    )
    return jax.shard_map(
        on_device, mesh=mesh, in_specs=in_specs, out_specs=P("group", "local"), check_vma=False
    )
```

```python
import jax
import jax.numpy as jnp
from jax import lax
from jax.experimental import pallas as pl
from jax.experimental.pallas import tpu as pltpu
from jax.sharding import PartitionSpec as P

MESH = pl.DeviceIdType.MESH
F32, BF16 = jnp.float32, jnp.bfloat16

NY, NZ, NX = 4, 8, 4
GROUPS = NY * NZ
TOK, TOP, CAP = 64, 8, 24
FEAT, HPART = 896, 256
DEV = 2 * NX
ROWS = GROUPS * CAP
CHUNKS = NZ
CROWS = NY * CAP
HALF = CROWS // 2
DISTANCE = (1, 7, 2, 6, 3, 5, 4, 0)
AHEAD = 2

RIGHT, LEFT, RIGHT2, LEFT2, SIBLING, OVER = range(6)
FAR = RIGHT2


def distance_of(chunk):
    found = 0
    for index, value in enumerate(DISTANCE):
        if value:
            found = found + jnp.where(chunk == index, value, 0)
    return found


def kernel(
    tokens_ref, routes_ref, affinity_ref, gate_hbm, up_hbm, down_hbm, out_ref,
    gate_ref, up_ref, down_ref, outgoing, landed, rows, hidden, results, returned, weight_of, total,
    weight_sem, sent_sem, landed_sem, back_sem, returned_sem, x_send, x_recv, h_send, h_recv,
):
    me_g, me_l = lax.axis_index("group"), lax.axis_index("local")
    y, z = me_g // NZ, lax.rem(me_g, NZ)
    x, core = me_l // 2, lax.rem(me_l, 2)
    right = lax.rem(x + 1, NX) * 2 + core
    left = lax.rem(x + NX - 1, NX) * 2 + core
    far = lax.rem(x + 2, NX) * 2 + core
    right_x, left_x, far_x = lax.rem(x + 1, NX), lax.rem(x + NX - 1, NX), lax.rem(x + 2, NX)
    sibling = x * 2 + 1 - core

    def wrap(value, size):
        return jnp.where(value >= size, value - size, value)

    def group_at(dy, dz):
        return wrap(y + dy, NY) * NZ + wrap(z + dz, NZ)

    barrier = pltpu.get_barrier_semaphore()
    for offset in range(1, GROUPS):
        pl.semaphore_signal(
            barrier, inc=1, device_id=(wrap(me_g + offset, GROUPS), me_l), device_id_type=MESH
        )
    for peer in (right, left, far, sibling):
        pl.semaphore_signal(barrier, inc=1, device_id=(me_g, peer), device_id_type=MESH)

    weights = [
        pltpu.make_async_copy(source.at[0], target, weight_sem.at[index])
        for index, (source, target) in enumerate(
            ((gate_hbm, gate_ref), (up_hbm, up_ref), (down_hbm, down_ref))
        )
    ]
    for copy in weights:
        copy.start()

    block = lax.broadcasted_iota(jnp.int32, (GROUPS, TOK), 0)
    dz_of = distance_of(block // NY)
    dy_of = block - (block // NY) * NY
    yy, zz = y + NY - dy_of, z + NZ - dz_of
    yy = jnp.where(yy >= NY, yy - NY, yy)
    zz = jnp.where(zz >= NZ, zz - NZ, zz)
    expert = yy * NZ + zz
    named = jnp.zeros((GROUPS, TOK), F32)
    gates = jnp.zeros((GROUPS, TOK), F32)
    for k in range(TOP):
        same = routes_ref[k : k + 1, :] == expert
        named = named + jnp.where(same, 1.0, 0.0)
        gates = gates + jnp.where(same, affinity_ref[k : k + 1, :], 0.0)
    before = lax.broadcasted_iota(jnp.int32, (TOK, TOK), 0) < lax.broadcasted_iota(jnp.int32, (TOK, TOK), 1)
    earlier = jnp.dot(named.astype(BF16), jnp.where(before, 1.0, 0.0).astype(BF16), preferred_element_type=F32)
    slot = jnp.where(named > 0.5, earlier, -1.0).astype(jnp.int32)
    place = lax.broadcasted_iota(jnp.int32, (GROUPS, CAP, TOK), 1)
    holds = slot[:, None, :] == place
    pick = jnp.where(holds, 1.0, 0.0).reshape(ROWS, TOK).astype(BF16)
    for at in range(0, GROUPS, 8):
        part = jnp.dot(pick[at * CAP : (at + 8) * CAP], tokens_ref[...], preferred_element_type=F32)
        outgoing[at : at + 8] = part.reshape(8, CAP, FEAT).astype(BF16)

    pl.semaphore_wait(barrier, GROUPS - 1 + 4)

    own = DISTANCE.index(0) * NY
    pltpu.make_async_copy(outgoing.at[own], landed.at[own], landed_sem.at[own // NY]).start()

    def dispatch(s, carry):
        dz, dy = distance_of(s // NY), lax.rem(s, NY)

        @pl.when(s != own)
        def _():
            pltpu.make_async_remote_copy(
                src_ref=outgoing.at[s],
                dst_ref=landed.at[s],
                send_sem=sent_sem.at[0],
                recv_sem=landed_sem.at[s // NY],
                device_id=(group_at(NY - dy - jnp.where(dy == 0, NY, 0), NZ - dz - jnp.where(dz == 0, NZ, 0)), me_l),
                device_id_type=MESH,
            ).start()

        return carry

    lax.fori_loop(0, GROUPS, dispatch, 0)

    spread = jnp.where(holds, gates[:, None, :], 0.0).reshape(ROWS, TOK)
    high = spread.astype(BF16)
    low = (spread - high.astype(F32)).astype(BF16)
    weight_of[...] = jnp.concatenate([high.astype(F32), low.astype(F32)], axis=1).reshape(
        CHUNKS, CROWS, 2 * TOK
    )
    total[...] = jnp.zeros_like(total)

    def ring(buffer, send, recv, kind, chunk):
        start = pl.multiple_of(chunk * CROWS, CROWS)
        slots, begin, count, target = {
            RIGHT: (x, 0, CROWS, right),
            LEFT: (x, 0, CROWS, left),
            RIGHT2: (left_x, 0, HALF, right),
            LEFT2: (right_x, HALF, HALF, left),
            SIBLING: (pl.ds(0, NX), 0, CROWS, sibling),
            OVER: (x, 0, CROWS, far),
        }[kind]
        piece = buffer.at[core, slots, pl.ds(start + begin, count)]
        return pltpu.make_async_remote_copy(
            src_ref=piece,
            dst_ref=piece,
            send_sem=send.at[kind],
            recv_sem=recv.at[FAR if kind in (LEFT2, OVER) else kind, chunk],
            device_id=(me_g, target),
            device_id_type=MESH,
        )

    def arrival(buffer, recv, kind, chunk):
        here = pl.ds(pl.multiple_of(chunk * CROWS, CROWS), CROWS)
        piece = {
            RIGHT: lambda: buffer.at[core, left_x, here],
            LEFT: lambda: buffer.at[core, right_x, here],
            FAR: lambda: buffer.at[core, far_x, here],
            SIBLING: lambda: buffer.at[1 - core, pl.ds(0, NX), here],
        }[kind]()
        pltpu.make_async_copy(piece, piece, recv.at[kind, chunk]).wait()

    x_ring, h_ring = (rows, x_send, x_recv), (hidden, h_send, h_recv)

    def begin_rows(chunk):
        blocks_of = landed.at[pl.ds(chunk * NY, NY)]
        pltpu.make_async_copy(blocks_of, blocks_of, landed_sem.at[chunk]).wait()
        blocks = blocks_of[...].astype(F32).reshape(CROWS, FEAT).astype(BF16)
        rows[core, x, pl.ds(pl.multiple_of(chunk * CROWS, CROWS), CROWS)] = blocks
        for kind in (RIGHT, LEFT):
            ring(*x_ring, kind, chunk).start()

    def second(kit, chunk):
        for kind, onward in ((RIGHT, RIGHT2), (LEFT, LEFT2)):
            arrival(kit[0], kit[2], kind, chunk)
            ring(*kit, onward, chunk).start()

    def third(kit, chunk):
        arrival(kit[0], kit[2], FAR, chunk)
        ring(*kit, SIBLING, chunk).start()

    def all_over(kit, chunk):
        for kind in (RIGHT, LEFT, FAR):
            arrival(kit[0], kit[2], kind, chunk)
        ring(*kit, SIBLING, chunk).start()

    def gathered(kit, chunk):
        arrival(kit[0], kit[2], SIBLING, chunk)

    def hidden_rows(chunk):
        here = pl.ds(pl.multiple_of(chunk * CROWS, CROWS), CROWS)
        gate = jnp.zeros((CROWS, HPART), F32)
        up = jnp.zeros((CROWS, HPART), F32)
        for pair in range(NX):
            lhs = jnp.concatenate([rows[0, pair, here], rows[1, pair, here]], axis=1)
            depth = slice(pair * 2 * FEAT, (pair + 1) * 2 * FEAT)
            gate = gate + jnp.dot(lhs, gate_ref[depth, :], preferred_element_type=F32)
            up = up + jnp.dot(lhs, up_ref[depth, :], preferred_element_type=F32)
        value = gate / (1.0 + jnp.exp(-gate)) * up
        hidden[core, x, here] = value.astype(BF16)

    def output_rows(chunk):
        here = pl.ds(pl.multiple_of(chunk * CROWS, CROWS), CROWS)
        lhs = jnp.concatenate([hidden[part % 2, part // 2, here] for part in range(DEV)], axis=1)
        value = jnp.dot(lhs, down_ref[...], preferred_element_type=F32)
        results[pl.ds(chunk * NY, NY)] = value.reshape(NY, CAP, FEAT).astype(BF16)

    def send_back(chunk):
        dz = distance_of(chunk)
        for dy in range(NY):
            s = chunk * NY + dy

            @pl.when(s != own)
            def _():
                pltpu.make_async_remote_copy(
                    src_ref=results.at[s],
                    dst_ref=returned.at[s],
                    send_sem=back_sem.at[0],
                    recv_sem=returned_sem.at[chunk],
                    device_id=(group_at(dy, dz), me_l),
                    device_id_type=MESH,
                ).start()

            if dy == 0:

                @pl.when(s == own)
                def _():
                    pltpu.make_async_copy(results.at[s], returned.at[s], returned_sem.at[chunk]).start()

    def combine(chunk):
        blocks_of = returned.at[pl.ds(chunk * NY, NY)]
        pltpu.make_async_copy(blocks_of, blocks_of, returned_sem.at[chunk]).wait()
        values = blocks_of[...].astype(F32).reshape(CROWS, FEAT).astype(BF16)
        both = lax.dot_general(
            weight_of[chunk].astype(BF16), values, (((0,), (0,)), ((), ())), preferred_element_type=F32
        )
        total[...] += both[:TOK] + both[TOK:]

    def early(chunk, carry):
        begin_rows(chunk)
        return carry

    lax.fori_loop(0, AHEAD, early, 0)

    def turn(i, carry):
        @pl.when((i >= 1) & (i < CHUNKS + 1))
        def _():
            third(x_ring, i - 1)

        @pl.when(i < CHUNKS)
        def _():
            second(x_ring, i)

        @pl.when(i >= 2)
        def _():
            all_over(h_ring, i - 2)

        @pl.when(i == 1)
        def _():
            weights[0].wait()
            weights[1].wait()

        @pl.when((i >= 1) & (i < CHUNKS + 1))
        def _():
            gathered(x_ring, i - 1)
            hidden_rows(i - 1)
            for kind in (RIGHT, LEFT, OVER):
                ring(*h_ring, kind, i - 1).start()

        @pl.when(i == 2)
        def _():
            weights[2].wait()

        @pl.when(i >= 2)
        def _():
            gathered(h_ring, i - 2)
            output_rows(i - 2)
            send_back(i - 2)

        @pl.when(i + AHEAD < CHUNKS)
        def _():
            begin_rows(i + AHEAD)

        return carry

    lax.fori_loop(0, CHUNKS + 2, turn, 0)

    def collect(chunk, carry):
        combine(chunk)
        return carry

    lax.fori_loop(0, CHUNKS, collect, 0)
    out_ref[...] = total[...].astype(BF16)

    half = pl.ds(0, ROWS // 2)
    for send, kind, piece in (
        (x_send, RIGHT, rows.at[core, x]),
        (x_send, LEFT, rows.at[core, x]),
        (x_send, RIGHT2, rows.at[core, left_x, half]),
        (x_send, LEFT2, rows.at[core, right_x, half]),
        (x_send, SIBLING, rows.at[core]),
        (h_send, RIGHT, hidden.at[core, x]),
        (h_send, LEFT, hidden.at[core, x]),
        (h_send, OVER, hidden.at[core, x]),
        (h_send, SIBLING, hidden.at[core]),
    ):
        pltpu.make_async_copy(piece, piece, send.at[kind]).wait()
    others = pl.ds(0, GROUPS - 1)
    pltpu.make_async_copy(outgoing.at[others], outgoing.at[others], sent_sem.at[0]).wait()
    pltpu.make_async_copy(results.at[others], results.at[others], back_sem.at[0]).wait()


def on_device(tokens, routes, affinity, gate_proj, up_proj, down_proj):
    vmem, anywhere = pl.BlockSpec(memory_space=pltpu.VMEM), pl.BlockSpec(memory_space=pl.ANY)
    dma = pltpu.SemaphoreType.DMA
    return pl.pallas_call(
        kernel,
        out_shape=pltpu.VMEM((TOK, FEAT), BF16),
        in_specs=[vmem, vmem, vmem, anywhere, anywhere, anywhere],
        out_specs=vmem,
        scratch_shapes=[
            pltpu.VMEM((DEV * FEAT, HPART), BF16),
            pltpu.VMEM((DEV * FEAT, HPART), BF16),
            pltpu.VMEM((DEV * HPART, FEAT), BF16),
            pltpu.VMEM((GROUPS, CAP, FEAT), BF16),
            pltpu.VMEM((GROUPS, CAP, FEAT), BF16),
            pltpu.VMEM((2, NX, ROWS, FEAT), BF16),
            pltpu.VMEM((2, NX, ROWS, HPART), BF16),
            pltpu.VMEM((GROUPS, CAP, FEAT), BF16),
            pltpu.VMEM((GROUPS, CAP, FEAT), BF16),
            pltpu.VMEM((CHUNKS, CROWS, 2 * TOK), F32),
            pltpu.VMEM((TOK, FEAT), F32),
            dma((3,)),
            dma((1,)),
            dma((CHUNKS,)),
            dma((1,)),
            dma((CHUNKS,)),
            dma((6,)),
            dma((6, CHUNKS)),
            dma((6,)),
            dma((6, CHUNKS)),
        ],
        compiler_params=pltpu.CompilerParams(
            collective_id=0, has_side_effects=True, vmem_limit_bytes=56 * 1024 * 1024
        ),
        cost_estimate=pl.CostEstimate(flops=8_500_000_000, bytes_accessed=11_500_000, transcendentals=200_000),
    )(tokens, routes.T, affinity.T, gate_proj, up_proj, down_proj)


def solution(mesh):
    in_specs = (
        P("group", "local"),
        P("group", None),
        P("group", None),
        P("group", None, "local"),
        P("group", None, "local"),
        P("group", None, "local"),
    )
    return jax.shard_map(
        on_device, mesh=mesh, in_specs=in_specs, out_specs=P("group", "local"), check_vma=False
    )
```
